256 devices in a mesh: dp: 8 (over z), expert: 32 (over x, y, core).
Axes of the slice: x: 4, y: 4, z: 8, core: 2. Of those that a mesh axis runs over, the one named last changes fastest.
Arguments:
- tokens: bfloat16 [12288, 2048], P(('dp', 'expert')), may hold values from -6 to 6
- tokens_dot: bfloat16 [12288, 2048], P(('dp', 'expert')), may hold values from -6 to 6
- router: bfloat16 [2048, 64], replicated, may hold values from -0.125 to 0.125
- router_dot: bfloat16 [2048, 64], replicated, may hold values from -0.125 to 0.125
- expert_ids: int32 [12288, 8], P(('dp', 'expert')), may hold values from 0 to 63, all different within a row; in each aligned block of 48 rows (0 to 47, 48 to 95, ...) at most 12 rows name the same one
- priority: int32 [12288], P(('dp', 'expert')), may hold values from 0 to 12287, each once
- w_gate: bfloat16 [64, 768, 2048], P('expert', 'dp'), may hold values from -0.125 to 0.125
- w_up: bfloat16 [64, 768, 2048], P('expert', 'dp'), may hold values from -0.125 to 0.125
- w_down: bfloat16 [64, 768, 2048], P('expert', 'dp'), may hold values from -0.21875 to 0.21875
Outputs:
- mixed: bfloat16 [12288, 2048], P(('dp', 'expert'))
- mixed_dot: bfloat16 [12288, 2048], P(('dp', 'expert'))
The draws below stay inside these ranges and needn't reach their ends.
Inputs may be any that keep to these rules, and one draw needn't show every extreme that they name: `expert_ids`: each token names 8 different experts; among the tokens of one device no expert is named more than 12 times, and exactly 12 times in some device. `priority`: each rank appears once.
All inputs are finite; a program needn't handle non-finite values.
Results may differ from the reference program's by a relative error of at most 0.0058.
Values may be sent and summed in bfloat16 or wider, within the bound.
A program may use at most 128 MiB of HBM per device.

```python
import math
import jax
import jax.numpy as jnp
import numpy as np
from jax import lax

D = 2048
FF = 768
TOP = 8
TOK_DEV = 48
EXPERTS = 64
TOKENS = 12288
MOST = 12
CAP = 192
N_DP = 8
N_EXPERT = 32


def shard_levels(stream_key, shape, shards, smallest, top_value):
    loudness, own = 1.0, jax.random.fold_in(stream_key, 6)
    for dim, blocks in shards:
        heights = jnp.exp(jax.random.uniform(jax.random.fold_in(own, dim), (blocks,), jnp.float32, smallest / len(shards), top_value / len(shards)))
        loudness = loudness * jnp.repeat(heights, shape[dim] // blocks).reshape([-1 if axis == dim else 1 for axis in range(len(shape))])
    return loudness


def deal_out(key, own, number, rows, number_of, top, reach, slope):
    sequence = jax.random.permutation(key, number_of)
    crowded, ordinary = portions_of(number_of, rows * top, reach, slope, True), portions_of(number_of, rows * top, reach, slope, False)
    places = jnp.arange(number_of)

    def named(lengths, offset_by):
        used = int((lengths > 0).sum())
        fixed = max(1, used // 4)
        shifted = fixed + (places - fixed + offset_by * (used - fixed)) % max(1, number_of - fixed)
        return jnp.zeros((number_of,), jnp.int32).at[sequence[jnp.where(places < fixed, places, shifted)]].set(jnp.asarray(lengths, jnp.int32))

    lengths = jnp.where(number % 4 == 0, named(crowded, number // 4), named(ordinary, number - number // 4 - 1))
    mixed = jax.random.permutation(jax.random.fold_in(own, 3), number_of)
    giver, sink = mixed[0:number_of // 2 * 2:2], mixed[1:number_of // 2 * 2:2]
    slack = jnp.minimum(lengths[giver] - 1, reach - lengths[sink]) // 2
    slack = jnp.where((giver == sequence[0]) | (sink == sequence[0]) | (lengths[sink] == 0), 0, jnp.maximum(slack, 0))
    shifted = jax.random.randint(jax.random.fold_in(own, 4), (number_of // 2,), 0, 1 << 20) % (slack + 1)
    lengths = lengths.at[giver].add(-shifted).at[sink].add(shifted)
    items = jnp.searchsorted(jnp.cumsum(lengths), jnp.arange(rows * top), side="right").astype(jnp.int32)
    grid = items.reshape(top, rows).T
    grid = grid[jax.random.permutation(jax.random.fold_in(own, 1), rows)]
    offset_by = jax.random.randint(jax.random.fold_in(own, 2), (rows, 1), 0, top)
    return jnp.take_along_axis(grid, (jnp.arange(top)[None, :] + offset_by) % top, axis=1)


def portions_of(amount, total, bound, lean, full):
    weights = [(1 << 20) // math.isqrt(grade ** lean) + 1 for grade in range(1, amount + 1)]
    largest = bound if full else min(bound, max(-(-total // amount), total * weights[0] // sum(weights)))
    least = 1 if total - largest >= amount - 1 else 0
    given, spare = [largest] + [least] * (amount - 1), total - largest - least * (amount - 1)
    while spare > 0:
        candidates = [i for i in range(1, amount) if given[i] < largest] or [i for i in range(1, amount) if given[i] < bound]
        mass, left = sum([weights[i] for i in candidates]), spare
        for i in candidates:
            more = min(bound - given[i], max(1, left * weights[i] // mass), spare)
            given[i] = given[i] + more
            spare = spare - more
    return np.array(given)


def scatter_about(rng, extent, width, reach, cuts=(), kind=jnp.bfloat16):
    level = shard_levels(rng, extent, cuts, -0.22, 0.18) if cuts else 1.0
    drawn = jax.random.normal(rng, extent, jnp.float32) * width * level
    return jnp.minimum(jnp.maximum(drawn, -reach), reach).astype(kind)


def setup_inputs(seed: int = 0) -> dict:
    splits = jax.random.split(jax.random.key(seed), 10)
    tokens = scatter_about(splits[0], (TOKENS, D), 1.0, 6.0, ((0, 256),))
    tokens_dot = scatter_about(splits[1], (TOKENS, D), 1.0, 6.0, ((0, 256),))
    router = scatter_about(splits[2], (D, EXPERTS), D ** -0.5, 0.125)
    router_dot = scatter_about(splits[3], (D, EXPERTS), D ** -0.5, 0.125)
    expert_ids_keys = jax.random.split(jax.random.fold_in(splits[4], 1), TOKENS // TOK_DEV)
    expert_ids_turns = jax.random.permutation(jax.random.fold_in(splits[4], 3), TOKENS // TOK_DEV)
    expert_ids = jax.vmap(lambda own, number: deal_out(jax.random.fold_in(splits[4], 2), own, number, TOK_DEV, EXPERTS, TOP, MOST, 2))(expert_ids_keys, expert_ids_turns).reshape((TOKENS, TOP))
    priority = jax.random.permutation(splits[5], TOKENS).astype(jnp.int32)
    w_gate = scatter_about(splits[6], (EXPERTS, FF, D), D ** -0.5, 0.125, ((0, 32), (1, 8)))
    w_up = scatter_about(splits[7], (EXPERTS, FF, D), D ** -0.5, 0.125, ((0, 32), (1, 8)))
    w_down = scatter_about(splits[8], (EXPERTS, FF, D), FF ** -0.5, 0.21875, ((0, 32), (1, 8)))
    return {"tokens": tokens, "tokens_dot": tokens_dot, "router": router, "router_dot": router_dot, "expert_ids": expert_ids, "priority": priority, "w_gate": w_gate, "w_up": w_up, "w_down": w_down}


def expert_apply(packed, gate_mat, up_mat, down_mat):
    primal = packed[:, :D]
    tangent = packed[:, D:]
    gate_p = jnp.dot(primal, gate_mat.T, preferred_element_type=jnp.float32)
    up_p = jnp.dot(primal, up_mat.T, preferred_element_type=jnp.float32)
    gate_t = jnp.dot(tangent, gate_mat.T, preferred_element_type=jnp.float32)
    up_t = jnp.dot(tangent, up_mat.T, preferred_element_type=jnp.float32)
    sigma = 1.0 / (1.0 + jnp.exp(-gate_p))
    act = (gate_p * sigma * up_p).astype(jnp.bfloat16)
    act_dot = (sigma * (1.0 + gate_p * (1.0 - sigma)) * gate_t * up_p + gate_p * sigma * up_t).astype(jnp.bfloat16)
    out_p = jnp.dot(act, down_mat, preferred_element_type=jnp.float32)
    out_t = jnp.dot(act_dot, down_mat, preferred_element_type=jnp.float32)
    return jnp.stack([out_p, out_t], axis=1).astype(jnp.bfloat16)


def reference(tokens, tokens_dot, router, router_dot, expert_ids, priority, w_gate, w_up, w_down):
    logits = jnp.dot(tokens, router, preferred_element_type=jnp.float32)
    logits_dot = jnp.dot(tokens_dot, router, preferred_element_type=jnp.float32) + jnp.dot(tokens, router_dot, preferred_element_type=jnp.float32)
    member = (expert_ids[:, :, None] == jnp.arange(EXPERTS, dtype=jnp.int32)[None, None, :]).astype(jnp.float32)
    sel = jnp.sum(member * logits[:, None, :], axis=2)
    sel_dot = jnp.sum(member * logits_dot[:, None, :], axis=2)
    expo = jnp.exp(sel)
    gates = expo / jnp.sum(expo, axis=1, keepdims=True)
    gates_dot = gates * (sel_dot - jnp.sum(gates * sel_dot, axis=1, keepdims=True))
    per_group = N_EXPERT * TOK_DEV

    def group_apply(items):
        tok_g, tan_g, ids_g, rank_g, gate_g, gdot_g = items
        member_g = (ids_g[:, :, None] == jnp.arange(EXPERTS, dtype=jnp.int32)[None, None, :]).astype(jnp.float32)
        chosen = jnp.sum(member_g, axis=1)
        earlier = (rank_g[None, :] < rank_g[:, None]).astype(jnp.float32)
        ahead_e = jnp.dot(earlier, chosen, precision=lax.Precision.HIGHEST)
        ahead = jnp.sum(member_g * ahead_e[:, None, :], axis=2).astype(jnp.int32)
        kept = ahead < CAP
        position = jnp.where(kept, ahead, CAP).astype(jnp.int32)
        owners = jnp.repeat(jnp.arange(per_group, dtype=jnp.int32), TOP)
        table = jnp.full((EXPERTS, CAP), per_group, jnp.int32).at[ids_g.reshape(-1), position.reshape(-1)].set(owners, mode="drop")
        stacked = jnp.concatenate([tok_g, tan_g], axis=1)
        padded = jnp.concatenate([stacked, jnp.zeros((1, 2 * D), tok_g.dtype)], axis=0)
        packed = padded[table]
        results = lax.map(lambda entry: expert_apply(*entry), (packed, w_gate, w_up, w_down))
        picked = results[ids_g, jnp.minimum(position, CAP - 1)].astype(jnp.float32)
        picked = jnp.where(kept[:, :, None, None], picked, 0.0)
        mixed_g = jnp.sum(gate_g[:, :, None] * picked[:, :, 0], axis=1)
        mdot_g = jnp.sum(gdot_g[:, :, None] * picked[:, :, 0] + gate_g[:, :, None] * picked[:, :, 1], axis=1)
        return mixed_g.astype(jnp.bfloat16), mdot_g.astype(jnp.bfloat16)

    mixed, mixed_dot = lax.map(group_apply, (
        tokens.reshape(N_DP, per_group, D), tokens_dot.reshape(N_DP, per_group, D),
        expert_ids.reshape(N_DP, per_group, TOP), priority.reshape(N_DP, per_group),
        gates.reshape(N_DP, per_group, TOP), gates_dot.reshape(N_DP, per_group, TOP)))
    return mixed.reshape(TOKENS, D), mixed_dot.reshape(TOKENS, D)
```

```python
import functools

import jax
import jax.numpy as jnp
from jax import lax
from jax.experimental import pallas as pl
from jax.experimental.pallas import tpu as pltpu
from jax.sharding import PartitionSpec as P

GRID = (4, 4, 2)
CAP = 192
PARTS = 4
LANES = 64
VMEM_BYTES = 66_500_000
F32 = jnp.float32
BF16 = jnp.bfloat16


def ring_order(pieces, hops, cost, latency):
    ready = {(p, 1): 0.0 for p in range(pieces)}
    clock, order, done = 0.0, [], {}
    while ready:
        there = sorted(k for k, t in ready.items() if t <= clock)
        if not there:
            clock = min(ready.values())
            continue
        p, h = there[0]
        del ready[(p, h)]
        order.append((clock, p, h))
        clock += cost[p] * (0.5 if h == hops else 1.0)
        if h < hops:
            ready[(p, h + 1)] = clock + latency
        else:
            done[p] = clock + latency
    return order, done


def body(nz, tok, tokd, rout, routd, ids, rank, wg, wu, wd, out, outd,
         g_all, u_all, d_all, t_all, m_all, x_all, hid, place, place_t, slot_g, yy, keep, xsum, rows,
         c_in, y_in2, y_in1, x_in2, x_in1,
         zs, zr, ts, tr, ms, mr, cs, cr, ys, yr, xs, xr, loc):
    nx, ny, nc = GRID
    me = lax.axis_index("expert")
    z = lax.axis_index("dp")
    c = lax.rem(me, nc)
    y = lax.rem(lax.div(me, nc), ny)
    x = lax.div(me, nc * ny)
    td, width = tok.shape
    units = wg.shape[1]
    ff = units * nz
    dq = width // PARTS
    qw = 2 * dq
    top = ids.shape[1]
    hops = nz // 2

    def dev(zz, xx, yc, cc):
        return {"dp": zz, "expert": (xx * ny + yc) * nc + cc}

    def step(v, by, n):
        return lax.rem(v + (by + n), n)

    z_nb = [dev(step(z, s, nz), x, y, c) for s in (1, -1)]
    x_nb = [dev(z, step(x, s, nx), y, c) for s in (1, -1)]
    y_nb = [dev(z, x, step(y, s, ny), c) for s in (1, -1)]
    sib = dev(z, x, y, 1 - c)

    partners = [sib] + (z_nb if nz > 1 else []) + (x_nb if nx > 1 else []) + (y_nb if ny > 1 else [])
    barrier = pltpu.get_barrier_semaphore()
    for p in partners:
        pl.semaphore_signal(barrier, inc=1, device_id=p, device_id_type=pl.DeviceIdType.MESH)
    pl.semaphore_wait(barrier, len(partners))

    sent = []

    def send(src, dst, ssem, rsem, device):
        copy = pltpu.make_async_remote_copy(
            src_ref=src, dst_ref=dst, send_sem=ssem, recv_sem=rsem,
            device_id=device, device_id_type=pl.DeviceIdType.MESH)
        copy.start()
        return copy

    def arrived(dst, ssem, rsem, device):
        pltpu.make_async_remote_copy(
            src_ref=dst, dst_ref=dst, send_sem=ssem, recv_sem=rsem,
            device_id=device, device_id_type=pl.DeviceIdType.MESH).wait_recv()

    half_units = units // 2

    def piece_own(p):
        if p < 4:
            return (wg, wu)[p % 2].at[p // 2]
        return wd.at[:, :, pl.ds((p - 4) * dq, dq)]

    def piece_view(p, zz):
        at = pl.ds(pl.multiple_of(zz * units, units), units)
        if p < 4:
            return (g_all, u_all)[p % 2].at[p // 2, at]
        return d_all.at[p - 4, :, at]

    def piece_half(p, zz, d):
        if p < 4:
            at = pl.ds(pl.multiple_of(zz * units + d * half_units, half_units), half_units)
            return (g_all, u_all)[p % 2].at[p // 2, at]
        return d_all.at[p - 4, d, pl.ds(pl.multiple_of(zz * units, units), units)]

    pieces = 4 + PARTS

    def own_copy(p):
        return pltpu.make_async_copy(piece_own(p), piece_view(p, z), loc.at[p])

    def z_send(p, h):
        for d in range(2):
            sign = (-1, 1)[d]
            if h == 1:
                src, dst = piece_own(p), piece_view(p, z)
            else:
                origin = step(z, sign * (h - 1), nz)
                arrived(piece_view(p, origin), zs.at[p, d, h - 2], zr.at[p, d, h - 2], z_nb[d])
                src = piece_view(p, origin) if h < hops else piece_half(p, origin, d)
                dst = src
            sent.append(send(src, dst, zs.at[p, d, h - 1], zr.at[p, d, h - 1], z_nb[d]))

    def z_done(p):
        own_copy(p).wait()
        if nz > 1:
            for d in range(2):
                origin = step(z, (-1, 1)[d] * hops, nz)
                arrived(piece_half(p, origin, d), zs.at[p, d, hops - 1], zr.at[p, d, hops - 1], z_nb[d])

    def gather_steps(buf, ssem, rsem, log):
        wide = buf.shape[-1] // 2

        def x_view(i):
            return buf.at[y, c, i]

        def x_half(i, d):
            return buf.at[y, c, i, :, pl.ds(d * wide, wide)]

        def y_view(i):
            return buf.at[i, c]

        def y_half(i, d):
            return buf.at[i, c, :, :, pl.ds(d * wide, wide)]

        def one(base, view, pos, nb):
            for d in range(2):
                log.append(send(view(pos), view(pos), ssem.at[base + d], rsem.at[base + d], nb[d]))

        def two(base, view, half, pos, n, nb):
            for d in range(2):
                origin = step(pos, (-1, 1)[d], n)
                arrived(view(origin), ssem.at[base + d], rsem.at[base + d], nb[d])
                log.append(send(half(origin, d), half(origin, d), ssem.at[base + 2 + d], rsem.at[base + 2 + d], nb[d]))

        def three(base, half, pos, n, nb):
            for d in range(2):
                origin = step(pos, (-2, 2)[d], n)
                arrived(half(origin, d), ssem.at[base + 2 + d], rsem.at[base + 2 + d], nb[d])

        def cross(k):
            i = step(y, (0, -1, 1, 2)[k], ny)
            log.append(send(buf.at[i, c], buf.at[i, c], ssem.at[8 + k], rsem.at[8 + k], sib))

        def x1():
            if nx > 1:
                one(0, x_view, x, x_nb)

        def x2():
            if nx > 1:
                two(0, x_view, x_half, x, nx, x_nb)

        def y1():
            if nx > 1:
                three(0, x_half, x, nx, x_nb)
            if ny > 1:
                one(4, y_view, y, y_nb)
            cross(0)

        def y2():
            if ny > 1:
                two(4, y_view, y_half, y, ny, y_nb)
                cross(1)
                cross(2)

        def y3():
            if ny > 1:
                three(4, y_half, y, ny, y_nb)
                cross(3)

        def end():
            for k in range(4 if ny > 1 else 1):
                i = step(y, (0, -1, 1, 2)[k], ny)
                arrived(buf.at[i, 1 - c], ssem.at[8 + k], rsem.at[8 + k], sib)

        return x1, x2, y1, y2, y3, end

    t_log, m_log = [], []
    t_steps = gather_steps(t_all, ts, tr, t_log)
    m_steps = gather_steps(m_all, ms, mr, m_log)

    def tokens_start():
        t_all[y, c, x, :, pl.ds(0, width)] = tok[...]
        t_all[y, c, x, :, pl.ds(width, width)] = tokd[...]
        t_steps[0]()

    def routing_start():
        logits = jnp.dot(tok[...], rout[...], preferred_element_type=F32)
        logits_dot = jnp.dot(tokd[...], rout[...], preferred_element_type=F32) + jnp.dot(
            tok[...], routd[...], preferred_element_type=F32)
        lane = lax.broadcasted_iota(jnp.int32, (td, LANES), 1)
        member = jnp.zeros((td, LANES), F32)
        for k in range(top):
            member = jnp.where(lane == ids[:, k:k + 1], 1.0, member)
        chosen = member > 0.5
        expo = jnp.where(chosen, jnp.exp(jnp.where(chosen, logits, 0.0)), 0.0)
        gates = expo / jnp.sum(expo, axis=1, keepdims=True)
        sel_dot = jnp.where(chosen, logits_dot, 0.0)
        gates_dot = jnp.where(chosen, gates * (sel_dot - jnp.sum(gates * sel_dot, axis=1, keepdims=True)), 0.0)
        own_rank = jnp.broadcast_to(rank[...].astype(F32), (td, LANES))
        m_all[y, c, x] = jnp.concatenate([gates, gates_dot, member, own_rank], axis=1)
        m_steps[0]()

    group = nc * nx * td
    slots = 2 * CAP

    def routing_rows():
        lane = lax.broadcasted_iota(jnp.int32, (group, 4 * LANES), 1)
        lane_s = lax.broadcasted_iota(jnp.int32, (group, 128), 1)

        @pl.loop(0, ny)
        def _(i):
            m = m_all[i].reshape(group, 4 * LANES)
            picked = jnp.zeros((group, 128), F32)
            columns = [3 * LANES] + [2 * LANES + 2 * me + e for e in range(2)]
            columns += [2 * me + e for e in range(2)] + [LANES + 2 * me + e for e in range(2)]
            for j, col in enumerate(columns):
                v = jnp.sum(jnp.where(lane == col, m, 0.0), axis=1, keepdims=True)
                picked = jnp.where(lane_s == j, v, picked)
            rows[i] = jnp.transpose(picked)[0:8]

    def routing_ahead():
        whole = jnp.concatenate([rows[i] for i in range(ny)], axis=1)
        rank_t = whole[0:1]
        ahead = jnp.zeros((8, ny * group), F32)
        for i in range(ny):
            rank_s = m_all[i].reshape(group, 4 * LANES)[:, 3 * LANES:3 * LANES + 1]
            lower = jnp.where(rank_s < rank_t, 1.0, 0.0).astype(BF16)
            ahead = ahead + jnp.dot(rows[i].astype(BF16), lower, preferred_element_type=F32)
        seat = lax.broadcasted_iota(jnp.int32, (CAP, ny * group), 0).astype(F32)
        for e in range(2):
            here = jnp.where(whole[1 + e:2 + e] > 0.5, ahead[1 + e:2 + e], -1.0)
            hit = here == seat
            place[pl.ds(e * CAP, CAP)] = jnp.where(hit, 1.0, 0.0).astype(BF16)
            for r in range(2):
                slot_g[r, e] = jnp.sum(jnp.where(hit, whole[3 + 2 * r + e:4 + 2 * r + e], 0.0), axis=1, keepdims=True)

    def routing_turn():
        for i in range(ny):
            block = place[:, pl.ds(i * group, group)].astype(F32)
            place_t[i] = jnp.transpose(block).astype(BF16).reshape(nc, nx * td, slots)

    col = min(256, width)

    def pack(r, lo, hi):
        @pl.loop(lo, hi)
        def _(n):
            at = pl.multiple_of(n * col, col)
            picked = t_all[:, :, :, :, pl.ds(pl.multiple_of(r * width + at, col), col)].reshape(ny * group, col)
            res = jnp.dot(place[...], picked, preferred_element_type=F32).astype(BF16)
            for e in range(2):
                x_all[e, r, :, pl.ds(at, col)] = res[e * CAP:(e + 1) * CAP]

    fcol = 256 if ff % 256 == 0 else ff
    nt = (((1,), (1,)), ((), ()))

    def hidden(e, n):
        at = pl.ds(n * fcol, fcol)
        both = x_all[e].reshape(slots, width)
        ga = lax.dot_general(both, g_all[e, at], nt, preferred_element_type=F32)
        ua = lax.dot_general(both, u_all[e, at], nt, preferred_element_type=F32)
        gp, gt, up, ut = ga[:CAP], ga[CAP:], ua[:CAP], ua[CAP:]
        sigma = 1.0 / (1.0 + jnp.exp(-gp))
        hid[e, 0, :, at] = (gp * sigma * up).astype(BF16)
        hid[e, 1, :, at] = (sigma * (1.0 + gp * (1.0 - sigma)) * gt * up + gp * sigma * ut).astype(BF16)

    back_log = []

    def down(q):
        for e in range(2):
            res = jnp.dot(hid[e].reshape(slots, ff), d_all[q, e], preferred_element_type=F32)
            prim, tang = res[:CAP], res[CAP:]
            g, gd = slot_g[0, e], slot_g[1, e]
            yy[pl.ds(e * CAP, CAP), pl.ds(0, dq)] = (g * prim).astype(BF16)
            yy[pl.ds(e * CAP, CAP), pl.ds(dq, dq)] = (gd * prim + g * tang).astype(BF16)

    y_turn = (2, 1, -1, 0) if ny > 1 else (0,)

    def give(q):
        cols = pl.ds(q * qw, qw)
        for k, by in enumerate(y_turn):
            i = step(y, by, ny)
            res = jnp.dot(place_t[i, 1 - c], yy[...], preferred_element_type=F32)
            t_all[i, 0, :, :, cols] = res.astype(BF16).reshape(nx, td, qw)
            back_log.append(send(t_all.at[i, 0, :, :, cols], c_in.at[q, i], cs.at[q, k], cr.at[q, k], sib))
        for by in y_turn:
            i = step(y, by, ny)
            res = jnp.dot(place_t[i, c], yy[...], preferred_element_type=F32)
            keep[q % 2, i] = res.reshape(nx, td, qw)

    def summed(q, by):
        i = step(y, by, ny)
        k = y_turn.index(by)
        arrived(c_in.at[q, i], cs.at[q, k], cr.at[q, k], sib)
        return keep[q % 2, i] + c_in[q, i].astype(F32)

    lo, hi = pl.ds(0, dq), pl.ds(dq, dq)

    def y_first(q):
        if ny == 1:
            return
        cols = q * qw
        t_all[0, 1, :, :, pl.ds(cols, qw)] = summed(q, 2).astype(BF16)
        for d in range(2):
            src = t_all.at[0, 1, :, :, pl.ds(cols + d * dq, dq)]
            back_log.append(send(src, y_in2.at[q, :, :, pl.ds(d * dq, dq)], ys.at[q, d], yr.at[q, d], y_nb[d]))

    def y_second(q):
        if ny == 1:
            return
        cols = q * qw
        for d in range(2):
            v = summed(q, (1, -1)[d])
            mine = t_all.at[1 + d, 1, :, :, pl.ds(cols, qw)]
            got = y_in2.at[q, :, :, pl.ds(d * dq, dq)]
            arrived(got, ys.at[q, d], yr.at[q, d], y_nb[d])
            a, b = v[:, :, :dq], v[:, :, dq:]
            if d == 0:
                a = a + got[...].astype(F32)
            else:
                b = b + got[...].astype(F32)
            t_all[1 + d, 1, :, :, pl.ds(cols, dq)] = a.astype(BF16)
            t_all[1 + d, 1, :, :, pl.ds(cols + dq, dq)] = b.astype(BF16)
            back_log.append(send(mine, y_in1.at[q, d], ys.at[q, 2 + d], yr.at[q, 2 + d], y_nb[d]))

    def y_third(q):
        v = summed(q, 0)
        if ny > 1:
            for d in range(2):
                arrived(y_in1.at[q, d], ys.at[q, 2 + d], yr.at[q, 2 + d], y_nb[d])
                v = v + y_in1[q, d].astype(F32)
        xsum[q % 2] = v
        if nx > 1:
            cols = q * qw
            t_all[ny - 1, 1, 0, :, pl.ds(cols, qw)] = xsum[q % 2, step(x, 2, nx)].astype(BF16)
            for d in range(2):
                src = t_all.at[ny - 1, 1, 0, :, pl.ds(cols + d * dq, dq)]
                back_log.append(send(src, x_in2.at[q, :, pl.ds(d * dq, dq)], xs.at[q, d], xr.at[q, d], x_nb[d]))

    def x_second(q):
        if nx == 1:
            return
        cols = q * qw
        for d in range(2):
            v = xsum[q % 2, step(x, (1, -1)[d], nx)]
            got = x_in2.at[q, :, pl.ds(d * dq, dq)]
            arrived(got, xs.at[q, d], xr.at[q, d], x_nb[d])
            a, b = v[:, :dq], v[:, dq:]
            if d == 0:
                a = a + got[...].astype(F32)
            else:
                b = b + got[...].astype(F32)
            t_all[ny - 1, 1, 1 + d, :, pl.ds(cols, dq)] = a.astype(BF16)
            t_all[ny - 1, 1, 1 + d, :, pl.ds(cols + dq, dq)] = b.astype(BF16)
            src = t_all.at[ny - 1, 1, 1 + d, :, pl.ds(cols, qw)]
            back_log.append(send(src, x_in1.at[q, d], xs.at[q, 2 + d], xr.at[q, 2 + d], x_nb[d]))

    def x_third(q):
        v = xsum[q % 2, x]
        if nx > 1:
            for d in range(2):
                arrived(x_in1.at[q, d], xs.at[q, 2 + d], xr.at[q, 2 + d], x_nb[d])
                v = v + x_in1[q, d].astype(F32)
        out[:, pl.ds(q * dq, dq)] = v[:, :dq].astype(BF16)
        outd[:, pl.ds(q * dq, dq)] = v[:, dq:].astype(BF16)

    def settle_tokens():
        for copy in t_log + m_log:
            copy.wait_send()

    plan = []

    def at(t, f, *a):
        plan.append((t, len(plan), f, a))

    tau = 9.0
    cost = [tau] * 4 + [2 * tau / PARTS] * PARTS
    if nz > 1:
        order, done = ring_order(pieces, hops, cost, 2.0)
    else:
        order, done = [], {p: 60.0 + 15.0 * p for p in range(pieces)}
    started = sum(1 for t, p, h in order if h == 1 and t <= tau)
    for t, p, h in order:
        at(-1.0 if h == 1 and t <= tau else t - 0.9 * tau / 2 if h == 1 else t - 0.1, z_send, p, h)
    for p in range(pieces):
        at(-0.5, lambda p: own_copy(p).start(), p)
    at(0.0, routing_start)
    at(0.5, tokens_start)
    at(5.0, m_steps[1])
    at(12.0, m_steps[2])
    at(13.0, t_steps[1])
    at(19.0, t_steps[2])
    at(19.5, m_steps[3])
    at(21.0, m_steps[4])
    at(24.0, m_steps[5])
    at(25.0, routing_rows)
    at(30.0, routing_ahead)
    at(40.0, routing_turn)
    at(55.0, t_steps[3])
    at(72.0, t_steps[4])
    at(77.0, t_steps[5])
    blocks = width // col
    for r in range(2):
        for s in range(0, blocks, 2):
            at(78.0 + 8.0 * r + s, pack, r, s, min(s + 2, blocks))
    ready = 94.0
    for e in range(2):
        when = max(ready, done[2 * e + 1])
        at(when, z_done, 2 * e)
        at(when, z_done, 2 * e + 1)
        for n in range(ff // fcol):
            at(when + 0.1 + n * 1.5, hidden, e, n)
        ready = when + 5.0
    at(ready, settle_tokens)
    for q in range(PARTS):
        when = max(done[4 + q], ready + (10.0 if q else 0.1))
        at(when, z_done, 4 + q)
        at(when + 0.01, down, q)
        at(when + 1.0, give, q)
        at(when + 5.0, y_first, q)
        at(when + 10.0, y_second, q)
        at(when + 19.0, y_third, q)
        at(when + 22.0, x_second, q)
        at(when + 25.0, x_third, q)
        ready = when
    for _, _, f, a in sorted(plan, key=lambda item: item[:2]):
        f(*a)
    for copy in sent + back_log:
        copy.wait_send()


def shards(nz, tokens, tokens_dot, router, router_dot, expert_ids, priority, w_gate, w_up, w_down):
    nx, ny, nc = GRID
    td, width = tokens.shape
    units = w_gate.shape[1]
    ff = units * nz
    dq = width // PARTS
    qw = 2 * dq
    hops = max(nz // 2, 1)
    pieces = 4 + PARTS
    vmem = pl.BlockSpec(memory_space=pltpu.VMEM)
    hbm = pl.BlockSpec(memory_space=pl.ANY)
    dma = pltpu.SemaphoreType.DMA
    shape = jax.ShapeDtypeStruct((td, width), BF16)
    group = nc * nx * td
    scratch = [
        pltpu.VMEM((2, ff, width), BF16),
        pltpu.VMEM((2, ff, width), BF16),
        pltpu.VMEM((PARTS, 2, ff, dq), BF16),
        pltpu.VMEM((ny, nc, nx, td, 2 * width), BF16),
        pltpu.VMEM((ny, nc, nx, td, 4 * LANES), F32),
        pltpu.VMEM((2, 2, CAP, width), BF16),
        pltpu.VMEM((2, 2, CAP, ff), BF16),
        pltpu.VMEM((2 * CAP, ny * group), BF16),
        pltpu.VMEM((ny, nc, nx * td, 2 * CAP), BF16),
        pltpu.VMEM((2, 2, CAP, 1), F32),
        pltpu.VMEM((2 * CAP, qw), BF16),
        pltpu.VMEM((2, ny, nx, td, qw), F32),
        pltpu.VMEM((2, nx, td, qw), F32),
        pltpu.VMEM((ny, 8, group), F32),
        pltpu.VMEM((PARTS, ny, nx, td, qw), BF16),
        pltpu.VMEM((PARTS, nx, td, qw), BF16),
        pltpu.VMEM((PARTS, 2, nx, td, qw), BF16),
        pltpu.VMEM((PARTS, td, qw), BF16),
        pltpu.VMEM((PARTS, 2, td, qw), BF16),
        dma((pieces, 2, hops)), dma((pieces, 2, hops)),
        dma((12,)), dma((12,)), dma((12,)), dma((12,)),
        dma((PARTS, 4)), dma((PARTS, 4)), dma((PARTS, 4)), dma((PARTS, 4)), dma((PARTS, 4)), dma((PARTS, 4)),
        dma((pieces,)),
    ]
    return pl.pallas_call(
        functools.partial(body, nz),
        out_shape=(shape, shape),
        in_specs=[vmem] * 6 + [hbm] * 3,
        out_specs=(vmem, vmem),
        scratch_shapes=scratch,
        compiler_params=pltpu.CompilerParams(
            collective_id=0, has_side_effects=True, vmem_limit_bytes=VMEM_BYTES),
    )(tokens, tokens_dot, router, router_dot, expert_ids, priority.reshape(td, 1), w_gate, w_up, w_down)


def solution(mesh):
    return jax.shard_map(
        functools.partial(shards, mesh.shape["dp"]),
        mesh=mesh,
        in_specs=(
            P(("dp", "expert"), None),
            P(("dp", "expert"), None),
            P(),
            P(),
            P(("dp", "expert"), None),
            P(("dp", "expert")),
            P("expert", "dp", None),
            P("expert", "dp", None),
            P("expert", "dp", None),
        ),
        out_specs=(P(("dp", "expert"), None), P(("dp", "expert"), None)),
        check_vma=False,
    )
```

```python
import functools

import jax
import jax.numpy as jnp
from jax import lax
from jax.experimental import pallas as pl
from jax.experimental.pallas import tpu as pltpu
from jax.sharding import PartitionSpec as P

GRID = (4, 4, 2)
CAP = 192
PARTS = 8
AHEAD = 2.0
DEEP = 4
LANES = 64
VMEM_BYTES = 66_500_000
F32 = jnp.float32
BF16 = jnp.bfloat16


def ring_order(first, pieces, hops, cost, latency):
    order = [(p, h) for h in range(1, hops) for p in range(first)]
    last = [(p, hops) for p in range(first)]
    for k in range(pieces - first + hops - 1):
        if k < hops - 1:
            order += last[k::hops - 1]
        order += [(first + k - h + 1, h) for h in range(1, hops + 1) if first <= first + k - h + 1 < pieces]
    clock, landed, timed = 0.0, {}, []
    for p, h in order:
        clock = max(clock, landed.get((p, h - 1), 0.0))
        timed.append((clock, p, h))
        clock += cost[p] * (0.5 if h == hops else 1.0)
        landed[p, h] = clock + latency
    return timed, {p: landed[p, hops] for p in range(pieces)}


def body(nz, tok, tokd, rout, routd, ids, rank, wg, wu, wd, out, outd,
         g_all, u_all, d_all, t_all, m_all, x_all, hid, place, place_t, slot_g, yy, keep, xsum, rows,
         c_in, a_in2, a_in1, b_in2, b_in1,
         zs, zr, ts, tr, ms, mr, cs, cr, rs, rr, loc):
    nx, ny, nc = GRID
    me = lax.axis_index("expert")
    z = lax.axis_index("dp")
    c = lax.rem(me, nc)
    y = lax.rem(lax.div(me, nc), ny)
    x = lax.div(me, nc * ny)
    td, width = tok.shape
    units = wg.shape[1]
    ff = units * nz
    dq = width // PARTS
    qw = 2 * dq
    top = ids.shape[0]
    hops = nz // 2

    def dev(zz, xx, yc, cc):
        return {"dp": zz, "expert": (xx * ny + yc) * nc + cc}

    def step(v, by, n):
        return lax.rem(v + (by + n), n)

    z_nb = [dev(step(z, s, nz), x, y, c) for s in (1, -1)]
    x_nb = [dev(z, step(x, s, nx), y, c) for s in (1, -1)]
    y_nb = [dev(z, x, step(y, s, ny), c) for s in (1, -1)]
    sib = dev(z, x, y, 1 - c)

    partners = [sib] + (z_nb if nz > 1 else []) + (x_nb if nx > 1 else []) + (y_nb if ny > 1 else [])
    barrier = pltpu.get_barrier_semaphore()
    for p in partners:
        pl.semaphore_signal(barrier, inc=1, device_id=p, device_id_type=pl.DeviceIdType.MESH)
    pl.semaphore_wait(barrier, len(partners))

    sent = []

    def send(src, dst, ssem, rsem, device):
        copy = pltpu.make_async_remote_copy(
            src_ref=src, dst_ref=dst, send_sem=ssem, recv_sem=rsem,
            device_id=device, device_id_type=pl.DeviceIdType.MESH)
        copy.start()
        return copy

    def arrived(dst, ssem, rsem, device):
        pltpu.make_async_remote_copy(
            src_ref=dst, dst_ref=dst, send_sem=ssem, recv_sem=rsem,
            device_id=device, device_id_type=pl.DeviceIdType.MESH).wait_recv()

    half_units = units // 2

    def piece_own(p):
        if p < 4:
            return (wg, wu)[p % 2].at[p // 2]
        return wd.at[:, :, pl.ds((p - 4) * dq, dq)]

    def piece_view(p, zz):
        at = pl.ds(pl.multiple_of(zz * units, units), units)
        if p < 4:
            return (g_all, u_all)[p % 2].at[p // 2, at]
        return d_all.at[p - 4, :, at]

    def piece_half(p, zz, d):
        if p < 4:
            at = pl.ds(pl.multiple_of(zz * units + d * half_units, half_units), half_units)
            return (g_all, u_all)[p % 2].at[p // 2, at]
        return d_all.at[p - 4, d, pl.ds(pl.multiple_of(zz * units, units), units)]

    pieces = 4 + PARTS

    def own_copy(p):
        return pltpu.make_async_copy(piece_own(p), piece_view(p, z), loc.at[p])

    def z_send(p, h):
        for d in range(2):
            sign = (-1, 1)[d]
            if h == 1:
                src, dst = piece_own(p), piece_view(p, z)
            else:
                origin = step(z, sign * (h - 1), nz)
                arrived(piece_view(p, origin), zs.at[p, d, h - 2], zr.at[p, d, h - 2], z_nb[d])
                src = piece_view(p, origin) if h < hops else piece_half(p, origin, d)
                dst = src
            sent.append(send(src, dst, zs.at[p, d, h - 1], zr.at[p, d, h - 1], z_nb[d]))

    def z_done(p):
        own_copy(p).wait()
        if nz > 1:
            for d in range(2):
                origin = step(z, (-1, 1)[d] * hops, nz)
                arrived(piece_half(p, origin, d), zs.at[p, d, hops - 1], zr.at[p, d, hops - 1], z_nb[d])

    nt = (((1,), (1,)), ((), ()))

    def gather_steps(buf, ssem, rsem, log, lo, size, y_leads):
        cols = pl.ds(lo, size)
        pos1, n1, nb1, pos2, n2, nb2 = (y, ny, y_nb, x, nx, x_nb) if y_leads else (x, nx, x_nb, y, ny, y_nb)

        def part(d):
            return cols if d is None else pl.ds(lo + d * (size // 2), size // 2)

        def view1(i, d=None):
            return buf.at[i, c, x, :, part(d)] if y_leads else buf.at[y, c, i, :, part(d)]

        def view2(i, d=None, core=c):
            return buf.at[:, core, i, :, part(d)] if y_leads else buf.at[i, core, :, :, part(d)]

        def one(base, view, pos, nb):
            for d in range(2):
                log.append(send(view(pos), view(pos), ssem.at[base + d], rsem.at[base + d], nb[d]))

        def two(base, view, pos, n, nb):
            for d in range(2):
                origin = step(pos, (-1, 1)[d], n)
                arrived(view(origin), ssem.at[base + d], rsem.at[base + d], nb[d])
                log.append(send(view(origin, d), view(origin, d), ssem.at[base + 2 + d], rsem.at[base + 2 + d], nb[d]))

        def three(base, view, pos, n, nb):
            for d in range(2):
                arrived(view(step(pos, (-2, 2)[d], n), d), ssem.at[base + 2 + d], rsem.at[base + 2 + d], nb[d])

        def cross(k):
            i = step(pos2, (0, -1, 1, 2)[k], n2)
            log.append(send(view2(i), view2(i), ssem.at[8 + k], rsem.at[8 + k], sib))

        def first_start():
            if n1 > 1:
                one(0, view1, pos1, nb1)

        def first_relay():
            if n1 > 1:
                two(0, view1, pos1, n1, nb1)

        def second_start():
            if n1 > 1:
                three(0, view1, pos1, n1, nb1)
            if n2 > 1:
                one(4, view2, pos2, nb2)
            cross(0)

        def second_relay():
            if n2 > 1:
                two(4, view2, pos2, n2, nb2)
                cross(1)
                cross(2)

        def second_end():
            if n2 > 1:
                three(4, view2, pos2, n2, nb2)
                cross(3)

        def end():
            for k in range(4 if n2 > 1 else 1):
                i = step(pos2, (0, -1, 1, 2)[k], n2)
                arrived(view2(i, None, 1 - c), ssem.at[8 + k], rsem.at[8 + k], sib)

        return first_start, first_relay, second_start, second_relay, second_end, end

    t_log, m_log = [], []
    t_steps = [gather_steps(t_all, ts.at[a], tr.at[a], t_log, a * width, width, a == 1) for a in range(2)]
    m_steps = gather_steps(m_all, ms, mr, m_log, 0, 4 * LANES, False)

    def tokens_step(k):
        for a in range(2):
            t_steps[a][k]()

    def tokens_start():
        t_all[y, c, x, :, pl.ds(0, width)] = tok[...]
        t_all[y, c, x, :, pl.ds(width, width)] = tokd[...]
        tokens_step(0)

    def routing_start():
        logits = lax.dot_general(tok[...], rout[...], nt, preferred_element_type=F32)
        logits_dot = lax.dot_general(tokd[...], rout[...], nt, preferred_element_type=F32) + lax.dot_general(
            tok[...], routd[...], nt, preferred_element_type=F32)
        high = lax.div(rank[...], 128)
        low = rank[...] - 128 * high
        lines = [ids[...].astype(F32), high.astype(F32), low.astype(F32), jnp.zeros((14 - top, td), F32)]
        lines = jnp.concatenate(lines, axis=0).astype(BF16)
        eye = lax.broadcasted_iota(jnp.int32, (td, td), 0) == lax.broadcasted_iota(jnp.int32, (td, td), 1)
        turned = lax.dot_general(jnp.where(eye, 1.0, 0.0).astype(BF16), lines, nt, preferred_element_type=F32)
        lane = lax.broadcasted_iota(jnp.int32, (td, LANES), 1).astype(F32)
        member = jnp.zeros((td, LANES), F32)
        for k in range(top):
            member = jnp.where(lane == turned[:, k:k + 1], 1.0, member)
        chosen = member > 0.5
        expo = jnp.where(chosen, jnp.exp(jnp.where(chosen, logits, 0.0)), 0.0)
        gates = expo / jnp.sum(expo, axis=1, keepdims=True)
        sel_dot = jnp.where(chosen, logits_dot, 0.0)
        gates_dot = jnp.where(chosen, gates * (sel_dot - jnp.sum(gates * sel_dot, axis=1, keepdims=True)), 0.0)
        own_rank = jnp.broadcast_to(turned[:, top:top + 1] * 128.0 + turned[:, top + 1:top + 2], (td, LANES))
        m_all[y, c, x] = jnp.concatenate([gates, gates_dot, member, own_rank], axis=1)
        m_steps[0]()

    group = nc * nx * td
    slots = 2 * CAP

    def routing_rows():
        lane = lax.broadcasted_iota(jnp.int32, (group, 4 * LANES), 1)
        lane_s = lax.broadcasted_iota(jnp.int32, (group, 128), 1)

        @pl.loop(0, ny)
        def _(i):
            m = m_all[i].reshape(group, 4 * LANES)
            picked = jnp.zeros((group, 128), F32)
            columns = [3 * LANES] + [2 * LANES + 2 * me + e for e in range(2)]
            columns += [2 * me + e for e in range(2)] + [LANES + 2 * me + e for e in range(2)]
            for j, col in enumerate(columns):
                v = jnp.sum(jnp.where(lane == col, m, 0.0), axis=1, keepdims=True)
                picked = jnp.where(lane_s == j, v, picked)
            rows[i] = jnp.transpose(picked)[0:8]

    def routing_ahead():
        whole = jnp.concatenate([rows[i] for i in range(ny)], axis=1)
        rank_t = whole[0:1]
        ahead = jnp.zeros((8, ny * group), F32)
        for i in range(ny):
            rank_s = m_all[i].reshape(group, 4 * LANES)[:, 3 * LANES:3 * LANES + 1]
            lower = jnp.where(rank_s < rank_t, 1.0, 0.0).astype(BF16)
            ahead = ahead + jnp.dot(rows[i].astype(BF16), lower, preferred_element_type=F32)
        seat = lax.broadcasted_iota(jnp.int32, (CAP, ny * group), 0).astype(F32)
        for e in range(2):
            here = jnp.where(whole[1 + e:2 + e] > 0.5, ahead[1 + e:2 + e], -1.0)
            hit = here == seat
            place[pl.ds(e * CAP, CAP)] = jnp.where(hit, 1.0, 0.0).astype(BF16)
            for r in range(2):
                slot_g[r, e] = jnp.sum(jnp.where(hit, whole[3 + 2 * r + e:4 + 2 * r + e], 0.0), axis=1, keepdims=True)

    def routing_turn():
        for i in range(ny):
            block = place[:, pl.ds(i * group, group)].astype(F32)
            place_t[i] = jnp.transpose(block).astype(BF16).reshape(nc, nx * td, slots)

    col = min(256, width)

    def pack(r, lo, hi):
        @pl.loop(lo, hi)
        def _(n):
            at = pl.multiple_of(n * col, col)
            picked = t_all[:, :, :, :, pl.ds(pl.multiple_of(r * width + at, col), col)].reshape(ny * group, col)
            res = jnp.dot(place[...], picked, preferred_element_type=F32).astype(BF16)
            for e in range(2):
                x_all[e, r, :, pl.ds(at, col)] = res[e * CAP:(e + 1) * CAP]

    fcol = 256 if ff % 256 == 0 else ff
    def hidden(e, n):
        at = pl.ds(n * fcol, fcol)
        both = x_all[e].reshape(slots, width)
        ga = lax.dot_general(both, g_all[e, at], nt, preferred_element_type=F32)
        ua = lax.dot_general(both, u_all[e, at], nt, preferred_element_type=F32)
        gp, gt, up, ut = ga[:CAP], ga[CAP:], ua[:CAP], ua[CAP:]
        sigma = 1.0 / (1.0 + jnp.exp(-gp))
        hid[e, 0, :, at] = (gp * sigma * up).astype(BF16)
        hid[e, 1, :, at] = (sigma * (1.0 + gp * (1.0 - sigma)) * gt * up + gp * sigma * ut).astype(BF16)

    back_log = []

    def down(q):
        for e in range(2):
            res = jnp.dot(hid[e].reshape(slots, ff), d_all[q, e], preferred_element_type=F32)
            prim, tang = res[:CAP], res[CAP:]
            g, gd = slot_g[0, e], slot_g[1, e]
            yy[pl.ds(e * CAP, CAP), pl.ds(0, dq)] = (g * prim).astype(BF16)
            yy[pl.ds(e * CAP, CAP), pl.ds(dq, dq)] = (gd * prim + g * tang).astype(BF16)

    y_turn = (2, 1, -1, 0) if ny > 1 else (0,)

    def give(q):
        cols = pl.ds(q * qw, qw)
        for k, by in enumerate(y_turn):
            i = step(y, by, ny)
            res = jnp.dot(place_t[i, 1 - c], yy[...], preferred_element_type=F32)
            t_all[i, 0, :, :, cols] = res.astype(BF16).reshape(nx, td, qw)
            back_log.append(send(t_all.at[i, 0, :, :, cols], c_in.at[q, i], cs.at[q, k], cr.at[q, k], sib))
        for by in y_turn:
            i = step(y, by, ny)
            res = jnp.dot(place_t[i, c], yy[...], preferred_element_type=F32)
            keep[q % DEEP, i] = res.reshape(nx, td, qw)

    def spot(a, k):
        return (y, x)[a ^ k], (ny, nx)[a ^ k], (y_nb, x_nb)[a ^ k]

    def meet(q):
        for k, by in enumerate(y_turn):
            i = step(y, by, ny)
            arrived(c_in.at[q, i], cs.at[q, k], cr.at[q, k], sib)
            keep[q % DEEP, i] = keep[q % DEEP, i] + c_in[q, i].astype(F32)

    hw = dq // 2

    def block(q, a, i):
        cols = pl.ds(a * dq, dq)
        return keep[q % DEEP, i, :, :, cols] if a == 0 else keep[q % DEEP, :, i, :, cols]

    def relay_out(v, stage, into, base, q, a, nb):
        stage[...] = v.astype(BF16)
        for d in range(2):
            at = (slice(None),) * (len(into.shape) - 1) + (pl.ds(d * hw, hw),)
            back_log.append(send(stage.at[at], into.at[at], rs.at[q, a, base + d], rr.at[q, a, base + d], nb[d]))

    def relay_on(v, stage, into2, into1, base, q, a, d, nb):
        at = (slice(None),) * (len(into2.shape) - 1) + (pl.ds(d * hw, hw),)
        got = into2.at[at]
        arrived(got, rs.at[q, a, base + d], rr.at[q, a, base + d], nb)
        halves = [v[..., :hw], v[..., hw:]]
        halves[d] = halves[d] + got[...].astype(F32)
        stage[...] = jnp.concatenate(halves, axis=-1).astype(BF16)
        back_log.append(send(stage, into1, rs.at[q, a, base + 2 + d], rr.at[q, a, base + 2 + d], nb))

    def relay_end(v, into1, base, q, a, nb):
        for d in range(2):
            arrived(into1.at[d], rs.at[q, a, base + 2 + d], rr.at[q, a, base + 2 + d], nb[d])
            v = v + into1[d].astype(F32)
        return v

    def stage(q, a, k):
        return t_all.at[k, 1, :, :, pl.ds(q * qw + a * dq, dq)]

    def stage2(q, a, k):
        return t_all.at[ny - 1, 1, k, :, pl.ds(q * qw + a * dq, dq)]

    def back_first(q):
        meet(q)
        for a in range(2):
            pos, n, nb = spot(a, 0)
            if n > 1:
                relay_out(block(q, a, step(pos, 2, n)), stage(q, a, 0), a_in2.at[q, a], 0, q, a, nb)

    def back_second(q):
        for a in range(2):
            pos, n, nb = spot(a, 0)
            if n > 1:
                for d in range(2):
                    relay_on(block(q, a, step(pos, (1, -1)[d], n)), stage(q, a, 1 + d), a_in2.at[q, a],
                             a_in1.at[q, a, d], 0, q, a, d, nb[d])

    def back_third(q):
        for a in range(2):
            pos, n, nb = spot(a, 0)
            v = block(q, a, pos)
            if n > 1:
                v = relay_end(v, a_in1.at[q, a], 0, q, a, nb)
            xsum[q % DEEP, a] = v
            pos, n, nb = spot(a, 1)
            if n > 1:
                relay_out(xsum[q % DEEP, a, step(pos, 2, n)], stage2(q, a, 0), b_in2.at[q, a], 4, q, a, nb)

    def back_fourth(q):
        for a in range(2):
            pos, n, nb = spot(a, 1)
            if n > 1:
                for d in range(2):
                    relay_on(xsum[q % DEEP, a, step(pos, (1, -1)[d], n)], stage2(q, a, 1 + d), b_in2.at[q, a],
                             b_in1.at[q, a, d], 4, q, a, d, nb[d])

    def back_fifth(q):
        for a in range(2):
            pos, n, nb = spot(a, 1)
            v = xsum[q % DEEP, a, pos]
            if n > 1:
                v = relay_end(v, b_in1.at[q, a], 4, q, a, nb)
            (out, outd)[a][:, pl.ds(q * dq, dq)] = v.astype(BF16)

    def settle_tokens():
        for copy in t_log + m_log:
            copy.wait_send()

    plan = []

    def at(t, f, *a):
        plan.append((t, len(plan), f, a))

    tau = 8.8
    cost = [tau] * 4 + [2 * tau / PARTS] * PARTS
    if nz > 1:
        order, done = ring_order(4, pieces, hops, cost, 2.0)
    else:
        order, done = [], {p: 60.0 + 8.0 * p for p in range(pieces)}
    for t, p, h in order:
        at(t - AHEAD - (5.0 if h == 1 and p >= 4 else 0.0), z_send, p, h)
    for p in range(pieces):
        at(0.1, lambda p: own_copy(p).start(), p)
    at(0.2, routing_start)
    at(0.3, tokens_start)
    for t, k in ((6.0, 1), (9.0, 2), (13.0, 3), (15.0, 4), (17.0, 5)):
        at(t, m_steps[k])
    for t, k in ((9.5, 1), (13.5, 2), (34.0, 3), (44.0, 4), (48.0, 5)):
        at(t, tokens_step, k)
    at(18.0, routing_rows)
    at(22.0, routing_ahead)
    at(28.0, routing_turn)
    blocks = width // col
    for r in range(2):
        for s in range(0, blocks, 2):
            at(49.0 + 4.0 * r + s, pack, r, s, min(s + 2, blocks))
    ready = 60.0
    for e in range(2):
        when = max(ready, done[2 * e], done[2 * e + 1])
        at(when, z_done, 2 * e)
        at(when, z_done, 2 * e + 1)
        for n in range(ff // fcol):
            at(when + 0.1 + n * 1.5, hidden, e, n)
        ready = when + 5.0
    at(ready, settle_tokens)
    turn = []
    for q in range(PARTS):
        turn.append(max(done[4 + q], ready + (3.0 if q else 0.1)))
        ready = turn[-1]
    for q in range(PARTS):
        at(turn[q], z_done, 4 + q)
        at(turn[q] + 0.1, down, q)
        at(turn[q] + 0.2, give, q)
        for f, later in ((back_first, 3.5), (back_second, 7.0), (back_third, 11.5), (back_fourth, 14.5), (back_fifth, 17.5)):
            at(turn[q] + later, f, q)
    for _, _, f, a in sorted(plan, key=lambda item: item[:2]):
        f(*a)
    for copy in sent + back_log:
        copy.wait_send()


def shards(nz, tokens, tokens_dot, router, router_dot, expert_ids, priority, w_gate, w_up, w_down):
    nx, ny, nc = GRID
    td, width = tokens.shape
    units = w_gate.shape[1]
    ff = units * nz
    dq = width // PARTS
    qw = 2 * dq
    hops = max(nz // 2, 1)
    pieces = 4 + PARTS
    vmem = pl.BlockSpec(memory_space=pltpu.VMEM)
    hbm = pl.BlockSpec(memory_space=pl.ANY)
    dma = pltpu.SemaphoreType.DMA
    shape = jax.ShapeDtypeStruct((td, width), BF16)
    group = nc * nx * td
    scratch = [
        pltpu.VMEM((2, ff, width), BF16),
        pltpu.VMEM((2, ff, width), BF16),
        pltpu.VMEM((PARTS, 2, ff, dq), BF16),
        pltpu.VMEM((ny, nc, nx, td, 2 * width), BF16),
        pltpu.VMEM((ny, nc, nx, td, 4 * LANES), F32),
        pltpu.VMEM((2, 2, CAP, width), BF16),
        pltpu.VMEM((2, 2, CAP, ff), BF16),
        pltpu.VMEM((2 * CAP, ny * group), BF16),
        pltpu.VMEM((ny, nc, nx * td, 2 * CAP), BF16),
        pltpu.VMEM((2, 2, CAP, 1), F32),
        pltpu.VMEM((2 * CAP, qw), BF16),
        pltpu.VMEM((DEEP, ny, nx, td, qw), F32),
        pltpu.VMEM((DEEP, 2, nx, td, dq), F32),
        pltpu.VMEM((ny, 8, group), F32),
        pltpu.VMEM((PARTS, ny, nx, td, qw), BF16),
        pltpu.VMEM((PARTS, 2, 4, td, dq), BF16),
        pltpu.VMEM((PARTS, 2, 2, 4, td, dq), BF16),
        pltpu.VMEM((PARTS, 2, td, dq), BF16),
        pltpu.VMEM((PARTS, 2, 2, td, dq), BF16),
        dma((pieces, 2, hops)), dma((pieces, 2, hops)),
        dma((2, 12)), dma((2, 12)), dma((12,)), dma((12,)),
        dma((PARTS, 4)), dma((PARTS, 4)), dma((PARTS, 2, 8)), dma((PARTS, 2, 8)),
        dma((pieces,)),
    ]
    return pl.pallas_call(
        functools.partial(body, nz),
        out_shape=(shape, shape),
        in_specs=[vmem] * 6 + [hbm] * 3,
        out_specs=(vmem, vmem),
        scratch_shapes=scratch,
        compiler_params=pltpu.CompilerParams(
            collective_id=0, has_side_effects=True, vmem_limit_bytes=VMEM_BYTES),
    )(tokens, tokens_dot, router.T, router_dot.T, expert_ids.T, priority.reshape(1, td), w_gate, w_up, w_down)


def solution(mesh):
    return jax.shard_map(
        functools.partial(shards, mesh.shape["dp"]),
        mesh=mesh,
        in_specs=(
            P(("dp", "expert"), None),
            P(("dp", "expert"), None),
            P(),
            P(),
            P(("dp", "expert"), None),
            P(("dp", "expert")),
            P("expert", "dp", None),
            P("expert", "dp", None),
            P("expert", "dp", None),
        ),
        out_specs=(P(("dp", "expert"), None), P(("dp", "expert"), None)),
        check_vma=False,
    )
```

```python
import functools

import jax
import jax.numpy as jnp
from jax import lax
from jax.experimental import pallas as pl
from jax.experimental.pallas import tpu as pltpu
from jax.sharding import PartitionSpec as P

GRID = (4, 4, 2)
CAP = 192
PARTS = 8
AHEAD = 2.0
DEEP = 4
LANES = 64
VMEM_BYTES = 66_500_000
F32 = jnp.float32
BF16 = jnp.bfloat16


def ring_order(first, pieces, hops, cost, latency):
    order = [(p, h) for h in range(1, hops) for p in range(first)]
    last = [(p, hops) for p in range(first)]
    for k in range(pieces - first + hops - 1):
        if k < hops - 1:
            order += last[k::hops - 1]
        order += [(first + k - h + 1, h) for h in range(1, hops + 1) if first <= first + k - h + 1 < pieces]
    if first == 4 and hops == 4 and pieces > 8:
        order = [(p, 1) for p in range(4)] + [(0, 2), (1, 2), (4, 1), (2, 2), (3, 2)]
        order += [(0, 3), (1, 3), (4, 2), (2, 3), (5, 1), (3, 3), (0, 4), (4, 3), (1, 4), (2, 4), (5, 2), (3, 4)]
        order += [(4, 4), (6, 1), (5, 3), (6, 2), (5, 4), (7, 1)]
        for k in range(6, pieces):
            order += [(p, h) for p, h in ((k, 3), (k + 1, 2), (k + 2, 1), (k, 4)) if p < pieces]
    clock, landed, timed = 0.0, {}, []
    for p, h in order:
        clock = max(clock, landed.get((p, h - 1), 0.0))
        timed.append((clock, p, h))
        clock += cost[p] * (0.5 if h == hops else 1.0)
        landed[p, h] = clock + latency
    return timed, {p: landed[p, hops] for p in range(pieces)}


def body(nz, tok, tokd, rout, routd, ids, rank, wg, wu, wd, out, outd,
         g_all, u_all, d_all, t_all, m_all, x_all, hid, place, place_t, slot_g, yy, keep, xsum, rows,
         c_in, a_in2, a_in1, b_in2, b_in1,
         zs, zr, ts, tr, ms, mr, cs, cr, rs, rr, loc):
    nx, ny, nc = GRID
    me = lax.axis_index("expert")
    z = lax.axis_index("dp")
    c = lax.rem(me, nc)
    y = lax.rem(lax.div(me, nc), ny)
    x = lax.div(me, nc * ny)
    td, width = tok.shape
    units = wg.shape[1]
    ff = units * nz
    dq = width // PARTS
    qw = 2 * dq
    top = ids.shape[0]
    hops = nz // 2

    def dev(zz, xx, yc, cc):
        return {"dp": zz, "expert": (xx * ny + yc) * nc + cc}

    def step(v, by, n):
        return lax.rem(v + (by + n), n)

    z_nb = [dev(step(z, s, nz), x, y, c) for s in (1, -1)]
    x_nb = [dev(z, step(x, s, nx), y, c) for s in (1, -1)]
    y_nb = [dev(z, x, step(y, s, ny), c) for s in (1, -1)]
    sib = dev(z, x, y, 1 - c)

    partners = [sib] + (z_nb if nz > 1 else []) + (x_nb if nx > 1 else []) + (y_nb if ny > 1 else [])
    barrier = pltpu.get_barrier_semaphore()
    for p in partners:
        pl.semaphore_signal(barrier, inc=1, device_id=p, device_id_type=pl.DeviceIdType.MESH)
    pl.semaphore_wait(barrier, len(partners))

    sent = []

    def send(src, dst, ssem, rsem, device):
        copy = pltpu.make_async_remote_copy(
            src_ref=src, dst_ref=dst, send_sem=ssem, recv_sem=rsem,
            device_id=device, device_id_type=pl.DeviceIdType.MESH)
        copy.start()
        return copy

    def arrived(dst, ssem, rsem, device):
        pltpu.make_async_remote_copy(
            src_ref=dst, dst_ref=dst, send_sem=ssem, recv_sem=rsem,
            device_id=device, device_id_type=pl.DeviceIdType.MESH).wait_recv()

    half_units = units // 2

    def piece_own(p):
        if p < 4:
            return (wg, wu)[p % 2].at[p // 2]
        return wd.at[:, :, pl.ds((p - 4) * dq, dq)]

    def piece_view(p, zz):
        at = pl.ds(pl.multiple_of(zz * units, units), units)
        if p < 4:
            return (g_all, u_all)[p % 2].at[p // 2, at]
        return d_all.at[p - 4, :, at]

    def piece_half(p, zz, d):
        if p < 4:
            at = pl.ds(pl.multiple_of(zz * units + d * half_units, half_units), half_units)
            return (g_all, u_all)[p % 2].at[p // 2, at]
        return d_all.at[p - 4, d, pl.ds(pl.multiple_of(zz * units, units), units)]

    pieces = 4 + PARTS

    def own_copy(p):
        return pltpu.make_async_copy(piece_own(p), piece_view(p, z), loc.at[p])

    def z_send(p, h):
        for d in range(2):
            sign = (-1, 1)[d]
            if h == 1:
                src, dst = piece_own(p), piece_view(p, z)
            else:
                origin = step(z, sign * (h - 1), nz)
                arrived(piece_view(p, origin), zs.at[p, d, h - 2], zr.at[p, d, h - 2], z_nb[d])
                src = piece_view(p, origin) if h < hops else piece_half(p, origin, d)
                dst = src
            sent.append(send(src, dst, zs.at[p, d, h - 1], zr.at[p, d, h - 1], z_nb[d]))

    def z_done(p):
        own_copy(p).wait()
        if nz > 1:
            for d in range(2):
                origin = step(z, (-1, 1)[d] * hops, nz)
                arrived(piece_half(p, origin, d), zs.at[p, d, hops - 1], zr.at[p, d, hops - 1], z_nb[d])

    nt = (((1,), (1,)), ((), ()))

    def gather_steps(buf, ssem, rsem, log, lo, size, y_leads):
        cols = pl.ds(lo, size)
        pos1, n1, nb1, pos2, n2, nb2 = (y, ny, y_nb, x, nx, x_nb) if y_leads else (x, nx, x_nb, y, ny, y_nb)

        def part(d):
            return cols if d is None else pl.ds(lo + d * (size // 2), size // 2)

        def view1(i, d=None):
            return buf.at[i, c, x, :, part(d)] if y_leads else buf.at[y, c, i, :, part(d)]

        def view2(i, d=None, core=c):
            return buf.at[:, core, i, :, part(d)] if y_leads else buf.at[i, core, :, :, part(d)]

        def one(base, view, pos, nb):
            for d in range(2):
                log.append(send(view(pos), view(pos), ssem.at[base + d], rsem.at[base + d], nb[d]))

        def two(base, view, pos, n, nb):
            for d in range(2):
                origin = step(pos, (-1, 1)[d], n)
                arrived(view(origin), ssem.at[base + d], rsem.at[base + d], nb[d])
                log.append(send(view(origin, d), view(origin, d), ssem.at[base + 2 + d], rsem.at[base + 2 + d], nb[d]))

        def three(base, view, pos, n, nb):
            for d in range(2):
                arrived(view(step(pos, (-2, 2)[d], n), d), ssem.at[base + 2 + d], rsem.at[base + 2 + d], nb[d])

        def cross(k):
            i = step(pos2, (0, -1, 1, 2)[k], n2)
            log.append(send(view2(i), view2(i), ssem.at[8 + k], rsem.at[8 + k], sib))

        def first_start():
            if n1 > 1:
                one(0, view1, pos1, nb1)

        def first_relay():
            if n1 > 1:
                two(0, view1, pos1, n1, nb1)

        def second_start():
            if n1 > 1:
                three(0, view1, pos1, n1, nb1)
            if n2 > 1:
                one(4, view2, pos2, nb2)
            cross(0)

        def second_relay():
            if n2 > 1:
                two(4, view2, pos2, n2, nb2)
                cross(1)
                cross(2)

        def second_end():
            if n2 > 1:
                three(4, view2, pos2, n2, nb2)
                cross(3)

        def end():
            for k in range(4 if n2 > 1 else 1):
                i = step(pos2, (0, -1, 1, 2)[k], n2)
                arrived(view2(i, None, 1 - c), ssem.at[8 + k], rsem.at[8 + k], sib)

        return first_start, first_relay, second_start, second_relay, second_end, end

    t_log, m_log = [], []
    t_steps = [gather_steps(t_all, ts.at[a], tr.at[a], t_log, a * width, width, a == 1) for a in range(2)]
    m_steps = gather_steps(m_all, ms, mr, m_log, 0, 4 * LANES, False)

    def tokens_step(k):
        for a in range(2):
            t_steps[a][k]()

    def tokens_start():
        t_all[y, c, x, :, pl.ds(0, width)] = tok[...]
        t_all[y, c, x, :, pl.ds(width, width)] = tokd[...]
        tokens_step(0)

    def routing_start():
        logits = lax.dot_general(tok[...], rout[...], nt, preferred_element_type=F32)
        logits_dot = lax.dot_general(tokd[...], rout[...], nt, preferred_element_type=F32) + lax.dot_general(
            tok[...], routd[...], nt, preferred_element_type=F32)
        high = lax.div(rank[...], 128)
        low = rank[...] - 128 * high
        lines = [ids[...].astype(F32), high.astype(F32), low.astype(F32), jnp.zeros((14 - top, td), F32)]
        lines = jnp.concatenate(lines, axis=0).astype(BF16)
        eye = lax.broadcasted_iota(jnp.int32, (td, td), 0) == lax.broadcasted_iota(jnp.int32, (td, td), 1)
        turned = lax.dot_general(jnp.where(eye, 1.0, 0.0).astype(BF16), lines, nt, preferred_element_type=F32)
        lane = lax.broadcasted_iota(jnp.int32, (td, LANES), 1).astype(F32)
        member = jnp.zeros((td, LANES), F32)
        for k in range(top):
            member = jnp.where(lane == turned[:, k:k + 1], 1.0, member)
        chosen = member > 0.5
        expo = jnp.where(chosen, jnp.exp(jnp.where(chosen, logits, 0.0)), 0.0)
        gates = expo / jnp.sum(expo, axis=1, keepdims=True)
        sel_dot = jnp.where(chosen, logits_dot, 0.0)
        gates_dot = jnp.where(chosen, gates * (sel_dot - jnp.sum(gates * sel_dot, axis=1, keepdims=True)), 0.0)
        own_rank = jnp.broadcast_to(turned[:, top:top + 1] * 128.0 + turned[:, top + 1:top + 2], (td, LANES))
        m_all[y, c, x] = jnp.concatenate([gates, gates_dot, member, own_rank], axis=1)
        m_steps[0]()

    group = nc * nx * td
    slots = 2 * CAP

    def routing_rows():
        lane = lax.broadcasted_iota(jnp.int32, (group, 4 * LANES), 1)
        lane_s = lax.broadcasted_iota(jnp.int32, (group, 128), 1)

        @pl.loop(0, ny)
        def _(i):
            m = m_all[i].reshape(group, 4 * LANES)
            picked = jnp.zeros((group, 128), F32)
            columns = [3 * LANES] + [2 * LANES + 2 * me + e for e in range(2)]
            columns += [2 * me + e for e in range(2)] + [LANES + 2 * me + e for e in range(2)]
            for j, col in enumerate(columns):
                v = jnp.sum(jnp.where(lane == col, m, 0.0), axis=1, keepdims=True)
                picked = jnp.where(lane_s == j, v, picked)
            rows[i] = jnp.transpose(picked)[0:8]

    def routing_ahead():
        whole = jnp.concatenate([rows[i] for i in range(ny)], axis=1)
        rank_t = whole[0:1]
        ahead = jnp.zeros((8, ny * group), F32)
        for i in range(ny):
            rank_s = m_all[i].reshape(group, 4 * LANES)[:, 3 * LANES:3 * LANES + 1]
            lower = jnp.where(rank_s < rank_t, 1.0, 0.0).astype(BF16)
            ahead = ahead + jnp.dot(rows[i].astype(BF16), lower, preferred_element_type=F32)
        seat = lax.broadcasted_iota(jnp.int32, (CAP, ny * group), 0).astype(F32)
        for e in range(2):
            here = jnp.where(whole[1 + e:2 + e] > 0.5, ahead[1 + e:2 + e], -1.0)
            hit = here == seat
            place[pl.ds(e * CAP, CAP)] = jnp.where(hit, 1.0, 0.0).astype(BF16)
            for r in range(2):
                slot_g[r, e] = jnp.sum(jnp.where(hit, whole[3 + 2 * r + e:4 + 2 * r + e], 0.0), axis=1, keepdims=True)

    def routing_turn():
        for i in range(ny):
            block = place[:, pl.ds(i * group, group)].astype(F32)
            place_t[i] = jnp.transpose(block).astype(BF16).reshape(nc, nx * td, slots)

    col = min(256, width)

    def pack(r, lo, hi):
        @pl.loop(lo, hi)
        def _(n):
            at = pl.multiple_of(n * col, col)
            picked = t_all[:, :, :, :, pl.ds(pl.multiple_of(r * width + at, col), col)].reshape(ny * group, col)
            res = jnp.dot(place[...], picked, preferred_element_type=F32).astype(BF16)
            for e in range(2):
                x_all[e, r, :, pl.ds(at, col)] = res[e * CAP:(e + 1) * CAP]

    fcol = 256 if ff % 256 == 0 else ff
    def hidden(e, n):
        at = pl.ds(n * fcol, fcol)
        both = x_all[e].reshape(slots, width)
        ga = lax.dot_general(both, g_all[e, at], nt, preferred_element_type=F32)
        ua = lax.dot_general(both, u_all[e, at], nt, preferred_element_type=F32)
        gp, gt, up, ut = ga[:CAP], ga[CAP:], ua[:CAP], ua[CAP:]
        sigma = 1.0 / (1.0 + jnp.exp(-gp))
        hid[e, 0, :, at] = (gp * sigma * up).astype(BF16)
        hid[e, 1, :, at] = (sigma * (1.0 + gp * (1.0 - sigma)) * gt * up + gp * sigma * ut).astype(BF16)

    back_log = []

    def down(q):
        for e in range(2):
            res = jnp.dot(hid[e].reshape(slots, ff), d_all[q, e], preferred_element_type=F32)
            prim, tang = res[:CAP], res[CAP:]
            g, gd = slot_g[0, e], slot_g[1, e]
            yy[pl.ds(e * CAP, CAP), pl.ds(0, dq)] = (g * prim).astype(BF16)
            yy[pl.ds(e * CAP, CAP), pl.ds(dq, dq)] = (gd * prim + g * tang).astype(BF16)

    y_turn = (2, 1, -1, 0) if ny > 1 else (0,)

    def give(q):
        cols = pl.ds(q * qw, qw)
        for k, by in enumerate(y_turn):
            i = step(y, by, ny)
            res = jnp.dot(place_t[i, 1 - c], yy[...], preferred_element_type=F32)
            t_all[i, 0, :, :, cols] = res.astype(BF16).reshape(nx, td, qw)
            back_log.append(send(t_all.at[i, 0, :, :, cols], c_in.at[q, i], cs.at[q, k], cr.at[q, k], sib))
        for by in y_turn:
            i = step(y, by, ny)
            res = jnp.dot(place_t[i, c], yy[...], preferred_element_type=F32)
            keep[q % DEEP, i] = res.reshape(nx, td, qw)

    def spot(a, k):
        return (y, x)[a ^ k], (ny, nx)[a ^ k], (y_nb, x_nb)[a ^ k]

    def meet(q):
        for k, by in enumerate(y_turn):
            i = step(y, by, ny)
            arrived(c_in.at[q, i], cs.at[q, k], cr.at[q, k], sib)
            keep[q % DEEP, i] = keep[q % DEEP, i] + c_in[q, i].astype(F32)

    hw = dq // 2

    def block(q, a, i):
        cols = pl.ds(a * dq, dq)
        return keep[q % DEEP, i, :, :, cols] if a == 0 else keep[q % DEEP, :, i, :, cols]

    def relay_out(v, stage, into, base, q, a, nb):
        stage[...] = v.astype(BF16)
        for d in range(2):
            at = (slice(None),) * (len(into.shape) - 1) + (pl.ds(d * hw, hw),)
            back_log.append(send(stage.at[at], into.at[at], rs.at[q, a, base + d], rr.at[q, a, base + d], nb[d]))

    def relay_on(v, stage, into2, into1, base, q, a, d, nb):
        at = (slice(None),) * (len(into2.shape) - 1) + (pl.ds(d * hw, hw),)
        got = into2.at[at]
        arrived(got, rs.at[q, a, base + d], rr.at[q, a, base + d], nb)
        halves = [v[..., :hw], v[..., hw:]]
        halves[d] = halves[d] + got[...].astype(F32)
        stage[...] = jnp.concatenate(halves, axis=-1).astype(BF16)
        back_log.append(send(stage, into1, rs.at[q, a, base + 2 + d], rr.at[q, a, base + 2 + d], nb))

    def relay_end(v, into1, base, q, a, nb):
        for d in range(2):
            arrived(into1.at[d], rs.at[q, a, base + 2 + d], rr.at[q, a, base + 2 + d], nb[d])
            v = v + into1[d].astype(F32)
        return v

    def stage(q, a, k):
        return t_all.at[k, 1, :, :, pl.ds(q * qw + a * dq, dq)]

    def stage2(q, a, k):
        return t_all.at[ny - 1, 1, k, :, pl.ds(q * qw + a * dq, dq)]

    def back_first(q):
        meet(q)
        for a in range(2):
            pos, n, nb = spot(a, 0)
            if n > 1:
                relay_out(block(q, a, step(pos, 2, n)), stage(q, a, 0), a_in2.at[q, a], 0, q, a, nb)

    def back_second(q):
        for a in range(2):
            pos, n, nb = spot(a, 0)
            if n > 1:
                for d in range(2):
                    relay_on(block(q, a, step(pos, (1, -1)[d], n)), stage(q, a, 1 + d), a_in2.at[q, a],
                             a_in1.at[q, a, d], 0, q, a, d, nb[d])

    def back_third(q):
        for a in range(2):
            pos, n, nb = spot(a, 0)
            v = block(q, a, pos)
            if n > 1:
                v = relay_end(v, a_in1.at[q, a], 0, q, a, nb)
            xsum[q % DEEP, a] = v
            pos, n, nb = spot(a, 1)
            if n > 1:
                relay_out(xsum[q % DEEP, a, step(pos, 2, n)], stage2(q, a, 0), b_in2.at[q, a], 4, q, a, nb)

    def back_fourth(q):
        for a in range(2):
            pos, n, nb = spot(a, 1)
            if n > 1:
                for d in range(2):
                    relay_on(xsum[q % DEEP, a, step(pos, (1, -1)[d], n)], stage2(q, a, 1 + d), b_in2.at[q, a],
                             b_in1.at[q, a, d], 4, q, a, d, nb[d])

    def back_fifth(q):
        for a in range(2):
            pos, n, nb = spot(a, 1)
            v = xsum[q % DEEP, a, pos]
            if n > 1:
                v = relay_end(v, b_in1.at[q, a], 4, q, a, nb)
            (out, outd)[a][:, pl.ds(q * dq, dq)] = v.astype(BF16)

    def settle_tokens():
        for copy in t_log + m_log:
            copy.wait_send()

    plan = []

    def at(t, f, *a):
        plan.append((t, len(plan), f, a))

    tau = 8.8
    cost = [tau] * 4 + [2 * tau / PARTS] * PARTS
    if nz > 1:
        order, done = ring_order(4, pieces, hops, cost, 2.0)
    else:
        order, done = [], {p: 60.0 + 8.0 * p for p in range(pieces)}
    for t, p, h in order:
        at(t - AHEAD - (5.0 if h == 1 and p >= 4 else 0.0), z_send, p, h)
    for p in range(pieces):
        at(0.1, lambda p: own_copy(p).start(), p)
    at(0.2, routing_start)
    at(0.3, tokens_start)
    for t, k in ((6.0, 1), (9.0, 2), (13.0, 3), (15.0, 4), (17.0, 5)):
        at(t, m_steps[k])
    for t, k in ((9.5, 1), (13.5, 2), (34.0, 3), (44.0, 4), (48.0, 5)):
        at(t, tokens_step, k)
    at(18.0, routing_rows)
    at(22.0, routing_ahead)
    at(28.0, routing_turn)
    blocks = width // col
    for r in range(2):
        for s in range(0, blocks, 2):
            at(49.0 + 4.0 * r + s, pack, r, s, min(s + 2, blocks))
    ready = 60.0
    for e in range(2):
        when = max(ready, done[2 * e], done[2 * e + 1])
        at(when, z_done, 2 * e)
        at(when, z_done, 2 * e + 1)
        for n in range(ff // fcol):
            at(when + 0.1 + n * 1.5, hidden, e, n)
        ready = when + 5.0
    at(ready, settle_tokens)
    turn = []
    for q in range(PARTS):
        turn.append(max(done[4 + q], ready + (4.5 if q else 0.1)))
        ready = turn[-1]
    for q in range(PARTS):
        at(turn[q], z_done, 4 + q)
        at(turn[q] + 0.1, down, q)
        at(turn[q] + 0.2, give, q)
        for f, later in ((back_first, 5.0), (back_second, 10.0), (back_third, 16.0), (back_fourth, 21.0), (back_fifth, 26.0)):
            at(turn[q] + later, f, q)
    for _, _, f, a in sorted(plan, key=lambda item: item[:2]):
        f(*a)
    for copy in sent + back_log:
        copy.wait_send()


def shards(nz, tokens, tokens_dot, router, router_dot, expert_ids, priority, w_gate, w_up, w_down):
    nx, ny, nc = GRID
    td, width = tokens.shape
    units = w_gate.shape[1]
    ff = units * nz
    dq = width // PARTS
    qw = 2 * dq
    hops = max(nz // 2, 1)
    pieces = 4 + PARTS
    vmem = pl.BlockSpec(memory_space=pltpu.VMEM)
    hbm = pl.BlockSpec(memory_space=pl.ANY)
    dma = pltpu.SemaphoreType.DMA
    shape = jax.ShapeDtypeStruct((td, width), BF16)
    group = nc * nx * td
    scratch = [
        pltpu.VMEM((2, ff, width), BF16),
        pltpu.VMEM((2, ff, width), BF16),
        pltpu.VMEM((PARTS, 2, ff, dq), BF16),
        pltpu.VMEM((ny, nc, nx, td, 2 * width), BF16),
        pltpu.VMEM((ny, nc, nx, td, 4 * LANES), F32),
        pltpu.VMEM((2, 2, CAP, width), BF16),
        pltpu.VMEM((2, 2, CAP, ff), BF16),
        pltpu.VMEM((2 * CAP, ny * group), BF16),
        pltpu.VMEM((ny, nc, nx * td, 2 * CAP), BF16),
        pltpu.VMEM((2, 2, CAP, 1), F32),
        pltpu.VMEM((2 * CAP, qw), BF16),
        pltpu.VMEM((DEEP, ny, nx, td, qw), F32),
        pltpu.VMEM((DEEP, 2, nx, td, dq), F32),
        pltpu.VMEM((ny, 8, group), F32),
        pltpu.VMEM((PARTS, ny, nx, td, qw), BF16),
        pltpu.VMEM((PARTS, 2, 4, td, dq), BF16),
        pltpu.VMEM((PARTS, 2, 2, 4, td, dq), BF16),
        pltpu.VMEM((PARTS, 2, td, dq), BF16),
        pltpu.VMEM((PARTS, 2, 2, td, dq), BF16),
        dma((pieces, 2, hops)), dma((pieces, 2, hops)),
        dma((2, 12)), dma((2, 12)), dma((12,)), dma((12,)),
        dma((PARTS, 4)), dma((PARTS, 4)), dma((PARTS, 2, 8)), dma((PARTS, 2, 8)),
        dma((pieces,)),
    ]
    return pl.pallas_call(
        functools.partial(body, nz),
        out_shape=(shape, shape),
        in_specs=[vmem] * 6 + [hbm] * 3,
        out_specs=(vmem, vmem),
        scratch_shapes=scratch,
        compiler_params=pltpu.CompilerParams(
            collective_id=0, has_side_effects=True, vmem_limit_bytes=VMEM_BYTES),
    )(tokens, tokens_dot, router.T, router_dot.T, expert_ids.T, priority.reshape(1, td), w_gate, w_up, w_down)


def solution(mesh):
    return jax.shard_map(
        functools.partial(shards, mesh.shape["dp"]),
        mesh=mesh,
        in_specs=(
            P(("dp", "expert"), None),
            P(("dp", "expert"), None),
            P(),
            P(),
            P(("dp", "expert"), None),
            P(("dp", "expert")),
            P("expert", "dp", None),
            P("expert", "dp", None),
            P("expert", "dp", None),
        ),
        out_specs=(P(("dp", "expert"), None), P(("dp", "expert"), None)),
        check_vma=False,
    )
```
